32 devices in a mesh: groups: 2 (over x), aux: 16 (over z, y, core).
Axes of the slice: x: 2, y: 2, z: 4, core: 2. Of those that a mesh axis runs over, the one named last changes fastest.
Arguments:
- integrals: bfloat16 [1024, 256, 256], P(('groups', 'aux')), parts along dimension 0, may hold values from -6 to 6
- coeffs: bfloat16 [512, 256], P('groups'), parts along dimension 0, may hold values from -0.375 to 0.375
- metric_inverse: bfloat16 [1024, 512], P('groups'), parts along dimension 0, may hold values from -3 to 3, as said below
- screen: int32 [8, 2, 2], P('groups'), parts along dimension 0, may hold values 0 or 1
Outputs:
- exchange: float32 [512, 256], P(('groups', 'aux')), parts along dimension 0
The draws below stay inside these ranges and needn't reach their ends.
There are 2 independent parts, one for each index of `groups`. The reference program is written for one: setup_inputs(seed, part) draws one part's arguments, and reference() takes and returns one part's arrays. A program takes and returns all parts, laid end to end along the dimension named above; each array names one. Nothing has to cross between parts.
Inputs may be any that keep to these rules, and one draw needn't show every extreme that they name: `metric_inverse`: symmetric, with diagonal entries between 0.5 and 2 and off-diagonal entries of size about 0.35·√2/√512; it is not guaranteed positive definite.
All inputs are finite; a program needn't handle non-finite values.
Results may differ from the reference program's by a relative error of at most 0.00033.
Values may be sent and summed in bfloat16 or wider, within the bound.
A program may use at most 128 MiB of HBM per device.

```python
import math
import jax
import jax.numpy as jnp
from jax import lax

TILE = 128
NB = 256
OCC = 256
AUX = 512


def draw_metric_inverse(key, part):
    key = jax.random.fold_in(key, 11)
    first, second = jax.random.split(key)
    raw = jnp.clip(jax.random.normal(first, (AUX, AUX), jnp.float32), -4.0, 4.0)
    spread = (raw + raw.T) * (0.35 / AUX ** 0.5)
    diagonal = jax.random.uniform(second, (AUX,), jnp.float32, 0.5, 2.0)
    eye_mask = (jnp.arange(AUX)[:, None] == jnp.arange(AUX)[None, :]).astype(jnp.float32)
    return (spread * (1.0 - eye_mask) + eye_mask * diagonal[None, :]).astype(jnp.bfloat16)


def touch_ends(array, key, least, high):
    extent = array.shape
    index_at = [jax.random.randint(jax.random.fold_in(key, axis), (), 0, extent[axis]) for axis in range(len(extent))]
    array = array.at[tuple(index_at)].set(least)
    longest = extent.index(max(extent))
    index_at[longest] = (index_at[longest] + 1) % extent[longest]
    return array.at[tuple(index_at)].set(high)


def levels(own_key, dims, pieces, smallest, high):
    gain, own = 1.0, jax.random.fold_in(own_key, 6)
    for position, shards_of in pieces:
        draws = jnp.exp(jax.random.uniform(jax.random.fold_in(own, position), (shards_of,), jnp.float32, smallest / len(pieces), high / len(pieces)))
        gain = gain * jnp.repeat(draws, dims[position] // shards_of).reshape([-1 if axis == position else 1 for axis in range(len(dims))])
    return gain


def centred(stream_key, dims, width, reach, shards=(), kind=jnp.bfloat16):
    array = jax.random.normal(stream_key, dims, jnp.float32) * width
    if len(shards) > 0:
        array = levels(stream_key, dims, shards, -0.22, 0.18) * array
    return jnp.clip(array, min=-reach, max=reach).astype(kind)


def setup_inputs(seed: int = 0, part: int = 0) -> dict:
    arg_keys = jax.random.split(jax.random.key(seed), 5)
    own_keys = jax.random.split(jax.random.fold_in(arg_keys[4], part), 5)
    integrals = centred(own_keys[0], (AUX, NB, NB), 1.0, 6.0, ((0, 16),))
    coeffs = centred(own_keys[1], (NB, OCC), NB ** -0.5, 0.375)
    metric_inverse = draw_metric_inverse(jax.random.fold_in(jax.random.fold_in(arg_keys[4], part), 71), part)
    screen = touch_ends((jax.random.randint(own_keys[3], (AUX // TILE, NB // TILE, OCC // TILE), 0, 4) < 3).astype(jnp.int32), jax.random.fold_in(own_keys[3], 1), 0, 1)
    return {"integrals": integrals, "coeffs": coeffs, "metric_inverse": metric_inverse, "screen": screen}


def reference(integrals, coeffs, metric_inverse, screen):
    tiles = AUX // TILE
    blocks = integrals.reshape(tiles, TILE, NB, NB)

    def half_block(pair):
        block, marks = pair
        prod = jnp.dot(block.reshape(TILE * NB, NB).astype(jnp.float32), coeffs.astype(jnp.float32), precision=lax.Precision.HIGHEST)
        prod = prod.reshape(TILE, NB // TILE, TILE, OCC // TILE, TILE)
        prod = prod * marks.astype(jnp.float32)[None, :, None, :, None]
        return prod.reshape(TILE, NB, OCC).astype(jnp.bfloat16)
    half = lax.map(half_block, (blocks, screen)).reshape(AUX, NB, OCC)
    metric_wide = metric_inverse.astype(jnp.float32)

    def accumulate_tile(total, index):
        piece = lax.dynamic_slice_in_dim(half, (index * TILE).astype(jnp.int32), TILE, 2).astype(jnp.float32)
        fitted_tensor = jnp.dot(metric_wide, piece.reshape(AUX, NB * TILE), precision=lax.Precision.HIGHEST)
        fitted_tensor = fitted_tensor.astype(jnp.bfloat16).astype(jnp.float32).reshape(AUX, NB, TILE)
        term = lax.dot_general(piece, fitted_tensor, (((0, 2), (0, 2)), ((), ())), precision=lax.Precision.HIGHEST)
        return (total + term, None)
    total, _ = lax.scan(accumulate_tile, jnp.zeros((NB, NB), jnp.float32), jnp.arange(OCC // TILE, dtype=jnp.int32))
    return total / math.sqrt(AUX * OCC)
```

```python
import functools
import math

import jax
import jax.numpy as jnp
from jax import lax
from jax.experimental import pallas as pl
from jax.experimental.pallas import tpu as pltpu
from jax.sharding import PartitionSpec as P

TILE = 128
GROUP = 16
MESH = pl.DeviceIdType.MESH


def peer(me, step, n):
    offset = n // 2 + ((step + 1) // 2) * (1 - 2 * (step % 2))
    return lax.rem(me + offset, n)


def kernel(
    n, chunk, integrals_hbm, coeffs_hbm, metric_hbm, screen_ref, out_ref,
    integrals, coeffs, coeffs_t, metric, stage, half, landed, total, blocks, parts,
    load_sem, send_sem, recv_sem, part_send_sem, part_recv_sem,
):
    me = lax.axis_index("aux")
    rows, basis, _ = integrals.shape
    occupied = coeffs.shape[1]
    aux = metric.shape[0]
    groups = rows // GROUP
    mine = occupied // n
    chunks = mine // chunk
    out_rows = basis // n
    scale = 1.0 / math.sqrt(aux * occupied)

    coeffs_copy = pltpu.make_async_copy(coeffs_hbm, coeffs, load_sem.at[0])
    metric_copy = pltpu.make_async_copy(metric_hbm, metric, load_sem.at[1])
    integral_copies = [
        pltpu.make_async_copy(
            integrals_hbm.at[pl.ds(g * GROUP, GROUP)],
            integrals.at[pl.ds(g * GROUP, GROUP)],
            load_sem.at[2 + g],
        )
        for g in range(groups)
    ]
    coeffs_copy.start()
    for copy in integral_copies:
        copy.start()
    metric_copy.start()

    barrier = pltpu.get_barrier_semaphore()

    @pl.loop(0, n - 1)
    def _(step):
        pl.semaphore_signal(
            barrier, inc=1, device_id={"aux": peer(me, step, n)}, device_id_type=MESH
        )

    tile = me * rows // TILE
    flags = [
        [screen_ref[tile, mt, it].astype(jnp.float32) for it in range(occupied // TILE)]
        for mt in range(basis // TILE)
    ]
    coeffs_copy.wait()
    coeffs_t[...] = coeffs[...].T

    def source(group, first, count, owner):
        return half.at[group, pl.ds(owner * mine + first, count)]

    def target(group, first, count, owner):
        start = pl.multiple_of(owner * rows + group * GROUP, GROUP)
        return landed.at[pl.ds(first, count), pl.ds(start, GROUP)]

    def transfer(unit, group, first, count, to, owner):
        return pltpu.make_async_remote_copy(
            src_ref=source(group, first, count, to),
            dst_ref=target(group, first, count, owner),
            send_sem=send_sem.at[unit, to],
            recv_sem=recv_sem.at[unit, owner],
            device_id={"aux": to},
            device_id_type=MESH,
        )

    units = [(g, 0, mine) for g in range(groups - 1)]
    units += [(groups - 1, c * chunk, chunk) for c in range(chunks)]

    for g in range(groups):
        integral_copies[g].wait()

        @pl.loop(0, GROUP)
        def _(p):
            product = lax.dot_general(
                coeffs_t[...], integrals[g * GROUP + p],
                (((1,), (1,)), ((), ())), preferred_element_type=jnp.float32,
            )
            for it in range(occupied // TILE):
                for mt in range(basis // TILE):
                    stage[mt, pl.ds(it * TILE * GROUP + p, TILE, stride=GROUP), :] = (
                        product[it * TILE:(it + 1) * TILE, mt * TILE:(mt + 1) * TILE] * flags[mt][it]
                    )

        def convert(owner):
            first = pl.multiple_of(owner * (mine * GROUP), mine * GROUP)
            block = stage[:, pl.ds(first, mine * GROUP), :].astype(jnp.bfloat16)
            return [part.reshape(mine, GROUP, TILE) for part in block]

        if g == 0:
            pl.semaphore_wait(barrier, n - 1)
        mine_units = [(u, unit) for u, unit in enumerate(units) if unit[0] == g]
        for index, (u, (_, first, count)) in enumerate(mine_units):
            @pl.loop(0, n - 1)
            def _(step):
                to = peer(me, step, n)
                if index == 0:
                    for mt, part in enumerate(convert(to)):
                        half[g, pl.ds(to * mine, mine), :, mt * TILE:(mt + 1) * TILE] = part
                transfer(u, g, first, count, to, me).start()

        start = pl.multiple_of(me * rows + g * GROUP, GROUP)
        for mt, part in enumerate(convert(me)):
            landed[:, pl.ds(start, GROUP), mt * TILE:(mt + 1) * TILE] = part

    metric_copy.wait()
    total[...] = jnp.zeros_like(total)

    def contract(i):
        depth = min(aux, 512)

        @pl.loop(0, aux // depth)
        def _(b):
            first = pl.multiple_of(b * depth, depth)
            fitted = jnp.dot(
                metric[pl.ds(first, depth), :], landed[i], preferred_element_type=jnp.float32
            ).astype(jnp.bfloat16)
            total[...] += lax.dot_general(
                landed[i, pl.ds(first, depth), :], fitted,
                (((0,), (0,)), ((), ())), preferred_element_type=jnp.float32,
            )

    for u, (g, first, count) in enumerate(units):
        @pl.loop(0, n - 1)
        def _(step):
            owner = peer(me, step, n)
            transfer(u, g, first, count, owner, owner).wait_recv()

        if g == groups - 1:
            pl.loop(first, first + count)(contract)

    for d in range(n):
        blocks[d] = total[d * out_rows:(d + 1) * out_rows, :]

    def part_transfer(to, owner):
        return pltpu.make_async_remote_copy(
            src_ref=blocks.at[to],
            dst_ref=parts.at[owner],
            send_sem=part_send_sem.at[to],
            recv_sem=part_recv_sem.at[owner],
            device_id={"aux": to},
            device_id_type=MESH,
        )

    @pl.loop(0, n - 1)
    def _(step):
        part_transfer(peer(me, step, n), me).start()

    parts[me] = blocks[me]

    @pl.loop(0, n - 1)
    def _(step):
        owner = peer(me, step, n)
        part_transfer(owner, owner).wait_recv()

    out_ref[...] = jnp.sum(parts[...], axis=0) * scale

    for u, (g, first, count) in enumerate(units):
        @pl.loop(0, n - 1)
        def _(step):
            to = peer(me, step, n)
            transfer(u, g, first, count, to, me).wait_send()

    @pl.loop(0, n - 1)
    def _(step):
        part_transfer(peer(me, step, n), me).wait_send()


def local(n, integrals, coeffs, metric_inverse, screen):
    rows, basis, _ = integrals.shape
    occupied = coeffs.shape[1]
    aux = metric_inverse.shape[0]
    mine = occupied // n
    chunk = min(4, mine)
    groups = rows // GROUP
    units = groups - 1 + mine // chunk
    out_rows = basis // n
    return pl.pallas_call(
        functools.partial(kernel, n, chunk),
        out_shape=jax.ShapeDtypeStruct((out_rows, basis), jnp.float32),
        in_specs=[pl.BlockSpec(memory_space=pl.ANY)] * 3 + [pl.BlockSpec(memory_space=pltpu.SMEM)],
        out_specs=pl.BlockSpec(memory_space=pltpu.VMEM),
        scratch_shapes=[
            pltpu.VMEM(integrals.shape, jnp.bfloat16),
            pltpu.VMEM(coeffs.shape, jnp.bfloat16),
            pltpu.VMEM((occupied, basis), jnp.bfloat16),
            pltpu.VMEM(metric_inverse.shape, jnp.bfloat16),
            pltpu.VMEM((basis // TILE, occupied * GROUP, TILE), jnp.float32),
            pltpu.VMEM((groups, occupied, GROUP, basis), jnp.bfloat16),
            pltpu.VMEM((mine, aux, basis), jnp.bfloat16),
            pltpu.VMEM((basis, basis), jnp.float32),
            pltpu.VMEM((n, out_rows, basis), jnp.float32),
            pltpu.VMEM((n, out_rows, basis), jnp.float32),
            pltpu.SemaphoreType.DMA((2 + groups,)),
            pltpu.SemaphoreType.DMA((units, n)),
            pltpu.SemaphoreType.DMA((units, n)),
            pltpu.SemaphoreType.DMA((n,)),
            pltpu.SemaphoreType.DMA((n,)),
        ],
        compiler_params=pltpu.CompilerParams(
            collective_id=0, has_side_effects=True, vmem_limit_bytes=48 * 1024 * 1024
        ),
        cost_estimate=pl.CostEstimate(
            flops=2 * basis * occupied * (rows * basis + aux * (aux + basis) // n),
            bytes_accessed=2 * (rows * basis * basis + aux * aux + basis * occupied),
            transcendentals=0,
        ),
    )(integrals, coeffs, metric_inverse, screen)


def solution(mesh):
    in_specs = (
        P(("groups", "aux"), None, None),
        P("groups", None),
        P("groups", None),
        P("groups", None, None),
    )
    out_specs = P(("groups", "aux"), None)
    return jax.shard_map(
        functools.partial(local, mesh.shape["aux"]),
        mesh=mesh, in_specs=in_specs, out_specs=out_specs, check_vma=False,
    )
```

```python
import functools
import math

import jax
import jax.numpy as jnp
from jax import lax
from jax.experimental import pallas as pl
from jax.experimental.pallas import tpu as pltpu
from jax.sharding import PartitionSpec as P

TILE = 128
GROUP = 16
MESH = pl.DeviceIdType.MESH


def peer(me, step, n):
    return lax.rem(me + step + 1, n)


def kernel(
    n, chunks, integrals_hbm, coeffs_hbm, metric_hbm, screen_ref, out_ref,
    integrals, coeffs, coeffs_t, metric, stage, half, landed, total, blocks, sibling_blocks, sums, parts,
    load_sem, send_sem, recv_sem, pair_send_sem, pair_recv_sem, part_send_sem, part_recv_sem,
):
    me = lax.axis_index("aux")
    rows, basis, _ = integrals.shape
    occupied = coeffs.shape[1]
    aux = metric.shape[0]
    groups = rows // GROUP
    mine = occupied // n
    out_rows = basis // n
    scale = 1.0 / math.sqrt(aux * occupied)

    coeffs_copy = pltpu.make_async_copy(coeffs_hbm, coeffs, load_sem.at[0])
    metric_copy = pltpu.make_async_copy(metric_hbm, metric, load_sem.at[1])
    integral_copies = [
        pltpu.make_async_copy(
            integrals_hbm.at[pl.ds(g * GROUP, GROUP)],
            integrals.at[pl.ds(g * GROUP, GROUP)],
            load_sem.at[2 + g],
        )
        for g in range(groups)
    ]
    coeffs_copy.start()
    for copy in integral_copies:
        copy.start()
    metric_copy.start()

    barrier = pltpu.get_barrier_semaphore()

    @pl.loop(0, n - 1)
    def _(step):
        pl.semaphore_signal(
            barrier, inc=1, device_id={"aux": peer(me, step, n)}, device_id_type=MESH
        )

    tile = me * rows // TILE
    flags = [
        [screen_ref[mt, it, tile].astype(jnp.float32) for it in range(occupied // TILE)]
        for mt in range(basis // TILE)
    ]
    coeffs_copy.wait()
    coeffs_t[...] = coeffs[...].T

    def source(group, first, count, owner):
        return half.at[group, pl.ds(owner * mine + first, count)]

    def target(group, first, count, owner):
        return landed.at[owner * groups + group, pl.ds(first, count)]

    def transfer(unit, group, first, count, to, owner):
        return pltpu.make_async_remote_copy(
            src_ref=source(group, first, count, to),
            dst_ref=target(group, first, count, owner),
            send_sem=send_sem.at[unit, to],
            recv_sem=recv_sem.at[unit, owner],
            device_id={"aux": to},
            device_id_type=MESH,
        )

    units = [(g, 0, mine) for g in range(groups - 1)]
    units += [(groups - 1, first, count) for first, count in chunks]

    for g in range(groups):
        integral_copies[g].wait()

        @pl.loop(0, GROUP, unroll=4)
        def _(p):
            product = lax.dot_general(
                coeffs_t[...], integrals[g * GROUP + p],
                (((1,), (1,)), ((), ())), preferred_element_type=jnp.float32,
            )
            for it in range(occupied // TILE):
                for mt in range(basis // TILE):
                    stage[mt, pl.ds(it * TILE * GROUP + p, TILE, stride=GROUP), :] = (
                        product[it * TILE:(it + 1) * TILE, mt * TILE:(mt + 1) * TILE] * flags[mt][it]
                    )

        def convert(owner):
            first = pl.multiple_of(owner * (mine * GROUP), mine * GROUP)
            block = stage[:, pl.ds(first, mine * GROUP), :].astype(jnp.bfloat16)
            return [part.reshape(mine, GROUP, TILE) for part in block]

        if g == 0:
            pl.semaphore_wait(barrier, n - 1)
        mine_units = [(u, unit) for u, unit in enumerate(units) if unit[0] == g]
        for index, (u, (_, first, count)) in enumerate(mine_units):
            @pl.loop(0, n - 1)
            def _(step):
                to = peer(me, step, n)
                if index == 0:
                    for mt, part in enumerate(convert(to)):
                        half[g, pl.ds(to * mine, mine), :, mt * TILE:(mt + 1) * TILE] = part
                transfer(u, g, first, count, to, me).start()

        for mt, part in enumerate(convert(me)):
            landed[me * groups + g, :, :, mt * TILE:(mt + 1) * TILE] = part

    metric_copy.wait()
    total[...] = jnp.zeros_like(total)

    def contract(i):
        depth = min(aux, 512)

        @pl.loop(0, aux // depth)
        def _(b):
            first = pl.multiple_of(b * depth, depth)
            fitted = jnp.dot(
                metric[pl.ds(first, depth), :], landed[:, i].reshape(aux, basis), preferred_element_type=jnp.float32
            ).astype(jnp.bfloat16)
            total[...] += lax.dot_general(
                landed[pl.ds(first // GROUP, depth // GROUP), i].reshape(depth, basis), fitted,
                (((0,), (0,)), ((), ())), preferred_element_type=jnp.float32,
            )

    for u, (g, first, count) in enumerate(units):
        @pl.loop(0, n - 1)
        def _(step):
            owner = peer(me, step, n)
            transfer(u, g, first, count, owner, owner).wait_recv()

        if g == groups - 1:
            pl.loop(first, first + count, unroll=min(count, 4))(contract)

    core, chip = lax.rem(me, 2), me // 2
    chips = n // 2
    for d in range(n):
        blocks[d % 2, d // 2] = total[d * out_rows:(d + 1) * out_rows, :]
    pair = pltpu.make_async_remote_copy(
        src_ref=blocks.at[1 - core],
        dst_ref=sibling_blocks,
        send_sem=pair_send_sem,
        recv_sem=pair_recv_sem,
        device_id={"aux": me + 1 - 2 * core},
        device_id_type=MESH,
    )
    pair.start()
    pair.wait_recv()
    sums[...] = blocks[core] + sibling_blocks[...]

    def part_transfer(to, owner):
        return pltpu.make_async_remote_copy(
            src_ref=sums.at[to],
            dst_ref=parts.at[owner],
            send_sem=part_send_sem.at[to],
            recv_sem=part_recv_sem.at[owner],
            device_id={"aux": 2 * to + core},
            device_id_type=MESH,
        )

    @pl.loop(0, chips - 1)
    def _(step):
        part_transfer(peer(chip, step, chips), chip).start()

    parts[chip] = sums[chip]

    @pl.loop(0, chips - 1)
    def _(step):
        owner = peer(chip, step, chips)
        part_transfer(owner, owner).wait_recv()

    out_ref[...] = jnp.sum(parts[...], axis=0) * scale

    for u, (g, first, count) in enumerate(units):
        @pl.loop(0, n - 1)
        def _(step):
            to = peer(me, step, n)
            transfer(u, g, first, count, to, me).wait_send()

    pair.wait_send()

    @pl.loop(0, chips - 1)
    def _(step):
        part_transfer(peer(chip, step, chips), chip).wait_send()


def local(n, integrals, coeffs, metric_inverse, screen):
    rows, basis, _ = integrals.shape
    occupied = coeffs.shape[1]
    aux = metric_inverse.shape[0]
    mine = occupied // n
    tail = max(mine // 4, 1)
    chunks = [(0, mine - tail), (mine - tail, tail)]
    groups = rows // GROUP
    units = groups - 1 + len(chunks)
    out_rows = basis // n
    return pl.pallas_call(
        functools.partial(kernel, n, chunks),
        out_shape=jax.ShapeDtypeStruct((out_rows, basis), jnp.float32),
        in_specs=[pl.BlockSpec(memory_space=pl.ANY)] * 3 + [pl.BlockSpec(memory_space=pltpu.SMEM)],
        out_specs=pl.BlockSpec(memory_space=pltpu.VMEM),
        scratch_shapes=[
            pltpu.VMEM(integrals.shape, jnp.bfloat16),
            pltpu.VMEM(coeffs.shape, jnp.bfloat16),
            pltpu.VMEM((occupied, basis), jnp.bfloat16),
            pltpu.VMEM(metric_inverse.shape, jnp.bfloat16),
            pltpu.VMEM((basis // TILE, occupied * GROUP, TILE), jnp.float32),
            pltpu.VMEM((groups, occupied, GROUP, basis), jnp.bfloat16),
            pltpu.VMEM((aux // GROUP, mine, GROUP, basis), jnp.bfloat16),
            pltpu.VMEM((basis, basis), jnp.float32),
            pltpu.VMEM((2, n // 2, out_rows, basis), jnp.float32),
            pltpu.VMEM((n // 2, out_rows, basis), jnp.float32),
            pltpu.VMEM((n // 2, out_rows, basis), jnp.float32),
            pltpu.VMEM((n // 2, out_rows, basis), jnp.float32),
            pltpu.SemaphoreType.DMA((2 + groups,)),
            pltpu.SemaphoreType.DMA((units, n)),
            pltpu.SemaphoreType.DMA((units, n)),
            pltpu.SemaphoreType.DMA,
            pltpu.SemaphoreType.DMA,
            pltpu.SemaphoreType.DMA((n // 2,)),
            pltpu.SemaphoreType.DMA((n // 2,)),
        ],
        compiler_params=pltpu.CompilerParams(
            collective_id=0, has_side_effects=True, vmem_limit_bytes=60 * 1024 * 1024
        ),
        cost_estimate=pl.CostEstimate(
            flops=2 * basis * occupied * (rows * basis + aux * (aux + basis) // n),
            bytes_accessed=2 * (rows * basis * basis + aux * aux + basis * occupied),
            transcendentals=0,
        ),
    )(integrals, coeffs, metric_inverse, jnp.transpose(screen, (1, 2, 0)))


def solution(mesh):
    in_specs = (
        P(("groups", "aux"), None, None),
        P("groups", None),
        P("groups", None),
        P("groups", None, None),
    )
    out_specs = P(("groups", "aux"), None)
    return jax.shard_map(
        functools.partial(local, mesh.shape["aux"]),
        mesh=mesh, in_specs=in_specs, out_specs=out_specs, check_vma=False,
    )
```

```python
import functools
import math

import jax
import jax.numpy as jnp
from jax import lax
from jax.experimental import pallas as pl
from jax.experimental.pallas import tpu as pltpu
from jax.sharding import PartitionSpec as P

TILE = 128
GROUP = 16
MESH = pl.DeviceIdType.MESH


def peer(me, step, n):
    return lax.rem(me + step + 1, n)


def kernel(
    n, chunks, integrals_hbm, coeffs_hbm, metric_hbm, screen_ref, out_ref,
    integrals, coeffs, coeffs_t, metric, stage, half, landed, total, blocks, sibling_blocks, sums, parts,
    load_sem, send_sem, recv_sem, pair_send_sem, pair_recv_sem, part_send_sem, part_recv_sem,
):
    me = lax.axis_index("aux")
    rows, basis, _ = integrals.shape
    occupied = coeffs.shape[1]
    aux = metric.shape[0]
    groups = rows // GROUP
    mine = occupied // n
    out_rows = basis // n
    scale = 1.0 / math.sqrt(aux * occupied)

    coeffs_copy = pltpu.make_async_copy(coeffs_hbm, coeffs, load_sem.at[0])
    metric_copy = pltpu.make_async_copy(metric_hbm, metric, load_sem.at[1])
    integral_copies = [
        pltpu.make_async_copy(
            integrals_hbm.at[pl.ds(g * GROUP, GROUP)],
            integrals.at[pl.ds(g * GROUP, GROUP)],
            load_sem.at[2 + g],
        )
        for g in range(groups)
    ]
    coeffs_copy.start()
    for copy in integral_copies:
        copy.start()
    metric_copy.start()

    barrier = pltpu.get_barrier_semaphore()

    @pl.loop(0, n - 1)
    def _(step):
        pl.semaphore_signal(
            barrier, inc=1, device_id={"aux": peer(me, step, n)}, device_id_type=MESH
        )

    tile = me * rows // TILE
    flags = [
        [screen_ref[mt, it, tile].astype(jnp.float32) for it in range(occupied // TILE)]
        for mt in range(basis // TILE)
    ]
    coeffs_copy.wait()
    coeffs_t[...] = coeffs[...].T

    def source(group, first, count, owner):
        return half.at[group, pl.ds(owner * mine + first, count)]

    def target(group, first, count, owner):
        return landed.at[owner * groups + group, pl.ds(first, count)]

    def transfer(unit, group, first, count, to, owner):
        return pltpu.make_async_remote_copy(
            src_ref=source(group, first, count, to),
            dst_ref=target(group, first, count, owner),
            send_sem=send_sem.at[unit, to],
            recv_sem=recv_sem.at[unit, owner],
            device_id={"aux": to},
            device_id_type=MESH,
        )

    units = [(g, 0, mine) for g in range(groups - 1)]
    units += [(groups - 1, first, count) for first, count in chunks]

    for g in range(groups):
        integral_copies[g].wait()

        @pl.loop(0, GROUP, unroll=4)
        def _(p):
            product = lax.dot_general(
                coeffs_t[...], integrals[g * GROUP + p],
                (((1,), (1,)), ((), ())), preferred_element_type=jnp.float32,
            )
            for it in range(occupied // TILE):
                for mt in range(basis // TILE):
                    stage[mt, pl.ds(it * TILE * GROUP + p, TILE, stride=GROUP), :] = (
                        product[it * TILE:(it + 1) * TILE, mt * TILE:(mt + 1) * TILE] * flags[mt][it]
                    )

        def convert(owner):
            first = pl.multiple_of(owner * (mine * GROUP), mine * GROUP)
            block = stage[:, pl.ds(first, mine * GROUP), :].astype(jnp.bfloat16)
            return [part.reshape(mine, GROUP, TILE) for part in block]

        if g == 0:
            @pl.loop(0, n - 1)
            def _(step):
                to = peer(me, step, n)
                for mt, part in enumerate(convert(to)):
                    half[g, pl.ds(to * mine, mine), :, mt * TILE:(mt + 1) * TILE] = part

            pl.semaphore_wait(barrier, n - 1)
        mine_units = [(u, unit) for u, unit in enumerate(units) if unit[0] == g]
        for index, (u, (_, first, count)) in enumerate(mine_units):
            @pl.loop(0, n - 1)
            def _(step):
                to = peer(me, step, n)
                if index == 0 and g > 0:
                    for mt, part in enumerate(convert(to)):
                        half[g, pl.ds(to * mine, mine), :, mt * TILE:(mt + 1) * TILE] = part
                transfer(u, g, first, count, to, me).start()

        for mt, part in enumerate(convert(me)):
            landed[me * groups + g, :, :, mt * TILE:(mt + 1) * TILE] = part

    metric_copy.wait()
    total[...] = jnp.zeros_like(total)

    def contract(i):
        depth = min(aux, 512)

        @pl.loop(0, aux // depth)
        def _(b):
            first = pl.multiple_of(b * depth, depth)
            fitted = jnp.dot(
                metric[pl.ds(first, depth), :], landed[:, i].reshape(aux, basis), preferred_element_type=jnp.float32
            ).astype(jnp.bfloat16)
            total[...] += lax.dot_general(
                landed[pl.ds(first // GROUP, depth // GROUP), i].reshape(depth, basis), fitted,
                (((0,), (0,)), ((), ())), preferred_element_type=jnp.float32,
            )

    for u, (g, first, count) in enumerate(units):
        @pl.loop(0, n - 1)
        def _(step):
            owner = peer(me, step, n)
            transfer(u, g, first, count, owner, owner).wait_recv()

        if g == groups - 1:
            pl.loop(first, first + count, unroll=min(count, 4))(contract)

    core, chip = lax.rem(me, 2), me // 2
    chips = n // 2
    for d in range(n):
        blocks[d % 2, d // 2] = total[d * out_rows:(d + 1) * out_rows, :]
    pair = pltpu.make_async_remote_copy(
        src_ref=blocks.at[1 - core],
        dst_ref=sibling_blocks,
        send_sem=pair_send_sem,
        recv_sem=pair_recv_sem,
        device_id={"aux": me + 1 - 2 * core},
        device_id_type=MESH,
    )
    pair.start()
    pair.wait_recv()
    sums[...] = blocks[core] + sibling_blocks[...]

    def part_transfer(to, owner):
        return pltpu.make_async_remote_copy(
            src_ref=sums.at[to],
            dst_ref=parts.at[owner],
            send_sem=part_send_sem.at[to],
            recv_sem=part_recv_sem.at[owner],
            device_id={"aux": 2 * to + core},
            device_id_type=MESH,
        )

    @pl.loop(0, chips - 1)
    def _(step):
        part_transfer(peer(chip, step, chips), chip).start()

    parts[chip] = sums[chip]

    @pl.loop(0, chips - 1)
    def _(step):
        owner = peer(chip, step, chips)
        part_transfer(owner, owner).wait_recv()

    out_ref[...] = jnp.sum(parts[...], axis=0) * scale

    for u, (g, first, count) in enumerate(units):
        @pl.loop(0, n - 1)
        def _(step):
            to = peer(me, step, n)
            transfer(u, g, first, count, to, me).wait_send()

    pair.wait_send()

    @pl.loop(0, chips - 1)
    def _(step):
        part_transfer(peer(chip, step, chips), chip).wait_send()


def local(n, integrals, coeffs, metric_inverse, screen):
    rows, basis, _ = integrals.shape
    occupied = coeffs.shape[1]
    aux = metric_inverse.shape[0]
    mine = occupied // n
    tail = max(mine // 4, 1)
    chunks = [(0, mine - tail), (mine - tail, tail)]
    groups = rows // GROUP
    units = groups - 1 + len(chunks)
    out_rows = basis // n
    return pl.pallas_call(
        functools.partial(kernel, n, chunks),
        out_shape=jax.ShapeDtypeStruct((out_rows, basis), jnp.float32),
        in_specs=[pl.BlockSpec(memory_space=pl.ANY)] * 3 + [pl.BlockSpec(memory_space=pltpu.SMEM)],
        out_specs=pl.BlockSpec(memory_space=pltpu.VMEM),
        scratch_shapes=[
            pltpu.VMEM(integrals.shape, jnp.bfloat16),
            pltpu.VMEM(coeffs.shape, jnp.bfloat16),
            pltpu.VMEM((occupied, basis), jnp.bfloat16),
            pltpu.VMEM(metric_inverse.shape, jnp.bfloat16),
            pltpu.VMEM((basis // TILE, occupied * GROUP, TILE), jnp.float32),
            pltpu.VMEM((groups, occupied, GROUP, basis), jnp.bfloat16),
            pltpu.VMEM((aux // GROUP, mine, GROUP, basis), jnp.bfloat16),
            pltpu.VMEM((basis, basis), jnp.float32),
            pltpu.VMEM((2, n // 2, out_rows, basis), jnp.float32),
            pltpu.VMEM((n // 2, out_rows, basis), jnp.float32),
            pltpu.VMEM((n // 2, out_rows, basis), jnp.float32),
            pltpu.VMEM((n // 2, out_rows, basis), jnp.float32),
            pltpu.SemaphoreType.DMA((2 + groups,)),
            pltpu.SemaphoreType.DMA((units, n)),
            pltpu.SemaphoreType.DMA((units, n)),
            pltpu.SemaphoreType.DMA,
            pltpu.SemaphoreType.DMA,
            pltpu.SemaphoreType.DMA((n // 2,)),
            pltpu.SemaphoreType.DMA((n // 2,)),
        ],
        compiler_params=pltpu.CompilerParams(
            collective_id=0, has_side_effects=True, vmem_limit_bytes=60 * 1024 * 1024
        ),
        cost_estimate=pl.CostEstimate(
            flops=2 * basis * occupied * (rows * basis + aux * (aux + basis) // n),
            bytes_accessed=2 * (rows * basis * basis + aux * aux + basis * occupied),
            transcendentals=0,
        ),
    )(integrals, coeffs, metric_inverse, jnp.transpose(screen, (1, 2, 0)))


def solution(mesh):
    in_specs = (
        P(("groups", "aux"), None, None),
        P("groups", None),
        P("groups", None),
        P("groups", None, None),
    )
    out_specs = P(("groups", "aux"), None)
    return jax.shard_map(
        functools.partial(local, mesh.shape["aux"]),
        mesh=mesh, in_specs=in_specs, out_specs=out_specs, check_vma=False,
    )
```
